32 devices in a mesh: groups: 2 (over x), dp: 16 (over z, y, core).
Axes of the slice: x: 2, y: 2, z: 4, core: 2. Of those that a mesh axis runs over, the one named last changes fastest.
Arguments:
- tokens: bfloat16 [8192, 8192], P(('groups', 'dp')), parts along dimension 0, may hold values from -6 to 6
- cotangent: bfloat16 [8192, 512], P(('groups', 'dp')), parts along dimension 0, may hold values from -1.5 to 1.5
- frozen_weight: bfloat16 [8192, 512], P('dp'), may hold values from -4 to 4
- frozen_scale: float32 [1], replicated, may hold values from 0.006 to 0.02
- adapter_down_weight: bfloat16 [128, 8192, 16], P('groups', 'dp'), parts along dimension 0, may hold values from -0.0625 to 0.0625
- adapter_up_weight: bfloat16 [128, 16, 512], P('groups'), parts along dimension 0, may hold values from -1.5 to 1.5
- sequence_adapter: int32 [64], P(('groups', 'dp')), parts along dimension 0, may hold values from 0 to 63
- sequence_token_length: int32 [64], P(('groups', 'dp')), parts along dimension 0, may hold values from 1 to 128, 2048 in all
Outputs:
- projection_output: bfloat16 [8192, 512], P(('groups', 'dp')), parts along dimension 0
- token_input_gradient: bfloat16 [8192, 8192], P(('groups', 'dp')), parts along dimension 0
- down_grad: float32 [128, 8192, 16], P('groups', 'dp'), parts along dimension 0
- adapter_up_gradient: float32 [128, 16, 512], P('groups', None, 'dp'), parts along dimension 0
The draws below stay inside these ranges and needn't reach their ends.
There are 2 independent parts, one for each index of `groups`. The reference program is written for one: setup_inputs(seed, part) draws one part's arguments, and reference() takes and returns one part's arrays. A program takes and returns all parts, laid end to end along the dimension named above; an argument that names none is the same for every part. Nothing has to cross between parts.
Inputs may be any that keep to these rules, and one draw needn't show every extreme that they name: `sequence_token_length`: within each independent job (one group), the 32 lengths sum to 2048 and the largest equals 128.
All inputs are finite; a program needn't handle non-finite values.
Results may differ from the reference program's by a relative error of at most 0.001.
The reference program's roundings to bfloat16 on the way count: a program that leaves them out, or rounds other values in their place, can miss the bound.
Values may be sent and summed in bfloat16 or wider, within the bound.
A program may use at most 128 MiB of HBM per device.

```python
import math
import jax
import jax.numpy as jnp
import numpy as np

MODEL_WIDTH = 8192
OUTPUT_FEATURES = 512
ADAPTER_COUNT = 64
ADAPTER_RANK = 16
SLOT = 128
SEQS = 32
TOKENS = 4096


def place_ends(entries, rng, smallest, top_value):
    place = [jax.random.randint(jax.random.fold_in(rng, axis), (), 0, length) for axis, length in enumerate(entries.shape)]
    main_axis = entries.shape.index(max(entries.shape))
    next_to = place[:main_axis] + [(place[main_axis] + 1) % entries.shape[main_axis]] + place[main_axis + 1:]
    return entries.at[tuple(place)].set(smallest).at[tuple(next_to)].set(top_value)


def steps_of(stream_key, shape, pieces, smallest, high):
    def one(position, parts):
        draws = jax.random.uniform(jax.random.fold_in(jax.random.fold_in(stream_key, 6), position), (parts,), jnp.float32, smallest / len(pieces), high / len(pieces))
        return jnp.repeat(jnp.exp(draws), shape[position] // parts).reshape((-1,) + (1,) * (len(shape) - position - 1))

    factor_of = one(*pieces[0])
    for cut in pieces[1:]:
        factor_of = factor_of * one(*cut)
    return factor_of


def rank_table(amount, skew):
    weights = [(1 << 20) // math.isqrt(grade ** skew) + 1 for grade in range(1, amount + 1)]
    deviation = 1 + sum(weights) // (1 << 30)
    return np.cumsum(np.array([max(1, weight // deviation) for weight in weights]))


def ranked_ids(key, dims, count, lean):
    table = rank_table(count, lean)
    ticket = jax.random.randint(jax.random.fold_in(key, 1), dims, 0, int(table[count - 1]))
    standing = jnp.searchsorted(jnp.asarray(table, jnp.int32), ticket, side="right")
    return jax.random.permutation(jax.random.fold_in(key, 2), count)[standing].astype(jnp.int32)


def profile(count, total, reach, lean):
    loads = [(1 << 20) // math.isqrt(grade ** lean) + 1 for grade in range(2, count + 1)]
    rest, given = total - reach - (count - 1), [1] * (count - 1)
    while rest > 0:
        candidates = [i for i in range(count - 1) if given[i] < reach]
        pool, budget = sum([loads[i] for i in candidates]), rest
        for i in candidates:
            extra = min(reach - given[i], max(1, budget * loads[i] // pool), rest)
            given[i] = given[i] + extra
            rest = rest - extra
    return np.array([reach] + given)


def uneven_parts(key, amount, total, bound, lean):
    if amount == 2:
        one = jax.random.randint(key, (), max(1, total - bound), min(bound, total - 1) + 1)
        return jnp.stack([one, total - one])
    lengths = jnp.asarray(profile(amount, total, bound, lean), jnp.int32)
    twos = (amount - 1) // 2
    donor, receiver = lengths[1:1 + 2 * twos:2], lengths[2:2 + 2 * twos:2]
    room = jnp.minimum(donor - 1, bound - receiver)
    passed = jax.random.randint(jax.random.fold_in(key, 1), (twos,), 0, 1 << 20) % (room + 1)
    lengths = lengths.at[1:1 + 2 * twos:2].set(donor - passed).at[2:2 + 2 * twos:2].set(receiver + passed)
    return lengths[jax.random.permutation(jax.random.fold_in(key, 2), amount)]


def centred(stream_key, shape, spread, most, pieces=(), held_as=jnp.bfloat16):
    entries = spread * jax.random.normal(stream_key, shape, jnp.float32)
    if pieces:
        entries = entries * steps_of(stream_key, shape, pieces, -0.22, 0.18)
    return jnp.clip(entries, -most, most).astype(held_as)


def setup_inputs(seed: int = 0, part: int = 0) -> dict:
    arg_keys = jax.random.split(jax.random.key(seed), 9)
    own_keys = jax.random.split(jax.random.fold_in(arg_keys[8], part), 9)
    tokens = centred(own_keys[0], (TOKENS, MODEL_WIDTH), 1.0, 6.0, ((0, 16),))
    cotangent = centred(own_keys[1], (TOKENS, OUTPUT_FEATURES), 0.25, 1.5, ((0, 16),))
    frozen_weight = centred(arg_keys[2], (MODEL_WIDTH, OUTPUT_FEATURES), 1.0, 4.0, ((0, 16),))
    frozen_scale = jnp.clip(jnp.exp(jax.random.uniform(arg_keys[3], (1,), jnp.float32, math.log(0.006), math.log(0.02))), 0.006, 0.02)
    adapter_down_weight = centred(own_keys[4], (ADAPTER_COUNT, MODEL_WIDTH, ADAPTER_RANK), MODEL_WIDTH ** -0.5, 0.0625, ((1, 16),))
    adapter_up_weight = centred(own_keys[5], (ADAPTER_COUNT, ADAPTER_RANK, OUTPUT_FEATURES), ADAPTER_RANK ** -0.5, 1.5)
    sequence_adapter = place_ends(ranked_ids(own_keys[6], (SEQS,), ADAPTER_COUNT, 2), jax.random.fold_in(own_keys[6], 3), 0, ADAPTER_COUNT - 1).astype(jnp.int32)
    sequence_token_length = uneven_parts(own_keys[7], SEQS, SEQS * SLOT // 2, SLOT, 2).astype(jnp.int32)
    return {"tokens": tokens, "cotangent": cotangent, "frozen_weight": frozen_weight, "frozen_scale": frozen_scale, "adapter_down_weight": adapter_down_weight, "adapter_up_weight": adapter_up_weight, "sequence_adapter": sequence_adapter, "sequence_token_length": sequence_token_length}


adapter_scale = 2.0


def reference(tokens, cotangent, frozen_weight, frozen_scale, adapter_down_weight, adapter_up_weight, sequence_adapter, sequence_token_length):
    scaling_factor = frozen_scale[0]
    token_ids = jnp.repeat(sequence_adapter, SLOT)
    positions = jnp.tile(jnp.arange(SLOT, dtype=jnp.int32), SEQS)
    valid_token_mask = positions < jnp.repeat(sequence_token_length, SLOT)
    adapter_onehot = token_ids[:, None] == jnp.arange(ADAPTER_COUNT, dtype=jnp.int32)[None, :]
    gathered_down_weight = jnp.transpose(adapter_down_weight, (1, 0, 2)).reshape(MODEL_WIDTH, ADAPTER_COUNT * ADAPTER_RANK)
    gathered_up_weight = adapter_up_weight.reshape(ADAPTER_COUNT * ADAPTER_RANK, OUTPUT_FEATURES)
    every_rank = jnp.dot(tokens, gathered_down_weight, preferred_element_type=jnp.float32).reshape(TOKENS, ADAPTER_COUNT, ADAPTER_RANK)
    rank_activations_rows = jnp.sum(jnp.where(adapter_onehot[:, :, None], every_rank, 0.0), axis=1).astype(jnp.bfloat16)
    rank_token_rows = jnp.where(adapter_onehot[:, :, None], rank_activations_rows[:, None, :], jnp.zeros((), jnp.bfloat16)).reshape(TOKENS, ADAPTER_COUNT * ADAPTER_RANK)
    frozen_output = jnp.dot(tokens, frozen_weight, preferred_element_type=jnp.float32)
    adapter_output = jnp.dot(rank_token_rows, gathered_up_weight, preferred_element_type=jnp.float32)
    projection_output = jnp.where(valid_token_mask[:, None], scaling_factor * frozen_output + adapter_scale * adapter_output, 0.0).astype(jnp.bfloat16)
    masked_cot = jnp.where(valid_token_mask[:, None], cotangent, jnp.zeros((), jnp.bfloat16))
    complete_up_gradient = jnp.dot(masked_cot, gathered_up_weight.T, preferred_element_type=jnp.float32).reshape(TOKENS, ADAPTER_COUNT, ADAPTER_RANK)
    rank_gradient = (adapter_scale * jnp.sum(jnp.where(adapter_onehot[:, :, None], complete_up_gradient, 0.0), axis=1)).astype(jnp.bfloat16)
    output_gradient_rows = jnp.where(adapter_onehot[:, :, None], rank_gradient[:, None, :], jnp.zeros((), jnp.bfloat16)).reshape(TOKENS, ADAPTER_COUNT * ADAPTER_RANK)
    adapter_input_grad = jnp.dot(output_gradient_rows, gathered_down_weight.T, preferred_element_type=jnp.float32).astype(jnp.bfloat16)
    frozen_input_grad = jnp.dot(masked_cot, frozen_weight.T, preferred_element_type=jnp.float32)
    token_input_gradient = (scaling_factor * frozen_input_grad + adapter_input_grad.astype(jnp.float32)).astype(jnp.bfloat16)
    down_flat = jnp.dot(tokens.T, output_gradient_rows, preferred_element_type=jnp.float32)
    down_grad = jnp.transpose(down_flat.reshape(MODEL_WIDTH, ADAPTER_COUNT, ADAPTER_RANK), (1, 0, 2))
    flattened_up_weight = jnp.dot(rank_token_rows.T, masked_cot, preferred_element_type=jnp.float32)
    adapter_up_gradient = adapter_scale * flattened_up_weight.reshape(ADAPTER_COUNT, ADAPTER_RANK, OUTPUT_FEATURES)
    return projection_output, token_input_gradient, down_grad, adapter_up_gradient
```

```python
import jax
import jax.numpy as jnp
from jax import lax
from jax.sharding import PartitionSpec as P

adapter_scale = 2.0


def local(
    tokens,
    cotangent,
    frozen_weight,
    frozen_scale,
    adapter_down_weight,
    adapter_up_weight,
    sequence_adapter,
    sequence_token_length,
):
    f32, bf16 = jnp.float32, jnp.bfloat16
    tok_count, width = tokens.shape
    seqs = sequence_adapter.shape[0]
    slot = tok_count // seqs
    adapters, shard_width, rank = adapter_down_weight.shape
    out_width = frozen_weight.shape[1]
    n = lax.axis_size("dp")
    scale = frozen_scale[0]

    every_index = lax.all_gather(sequence_adapter, "dp", axis=0, tiled=True)
    total = every_index.shape[0]
    weight = lax.all_gather(frozen_weight, "dp", axis=0, tiled=True)

    down_t = jnp.swapaxes(adapter_down_weight, 1, 2)
    chosen = down_t[every_index].reshape(total * rank, shard_width)
    own_down = lax.all_to_all(chosen, "dp", split_axis=0, concat_axis=1, tiled=True)
    own_down = own_down.reshape(seqs, rank, width)

    positions = lax.broadcasted_iota(jnp.int32, (seqs, slot), 1)
    live = (positions < sequence_token_length[:, None])[:, :, None]
    masked_cot = jnp.where(
        live, cotangent.reshape(seqs, slot, out_width), jnp.zeros((), bf16)
    )
    own_up = adapter_up_weight[sequence_adapter]
    grad_rank = (
        adapter_scale
        * jnp.einsum("spo,sro->spr", masked_cot, own_up, preferred_element_type=f32)
    ).astype(bf16)
    tokens_seq = tokens.reshape(seqs, slot, width)

    down_terms = jnp.einsum(
        "spr,spc->src", grad_rank, tokens_seq, preferred_element_type=f32
    )
    down_all = lax.all_to_all(
        down_terms.reshape(seqs * rank, width), "dp", split_axis=1, concat_axis=0, tiled=True
    )

    rank_vals = jnp.einsum(
        "spc,src->spr", tokens_seq, own_down, preferred_element_type=f32
    ).astype(bf16)
    up_terms = jnp.einsum(
        "spr,spo->sro", rank_vals, masked_cot, preferred_element_type=f32
    )
    up_all = lax.all_to_all(
        up_terms.reshape(seqs * rank, out_width), "dp", split_axis=1, concat_axis=0, tiled=True
    )

    select = (every_index[None, :] == jnp.arange(adapters, dtype=jnp.int32)[:, None]).astype(f32)
    down_grad = jnp.dot(
        select, down_all.reshape(total, rank * shard_width), precision=lax.Precision.HIGHEST
    ).reshape(adapters, rank, shard_width)
    down_grad = jnp.swapaxes(down_grad, 1, 2)
    up_grad = (
        adapter_scale
        * jnp.dot(
            select, up_all.reshape(total, rank * (out_width // n)), precision=lax.Precision.HIGHEST
        )
    ).reshape(adapters, rank, out_width // n)

    adapter_out = jnp.einsum("spr,sro->spo", rank_vals, own_up, preferred_element_type=f32)
    base_out = jnp.dot(tokens, weight, preferred_element_type=f32)
    combined = scale * base_out.reshape(seqs, slot, out_width) + adapter_scale * adapter_out
    projection = jnp.where(live, combined, 0.0).astype(bf16).reshape(tok_count, out_width)

    lora_back = jnp.einsum("spr,src->spc", grad_rank, own_down, preferred_element_type=f32).astype(bf16)
    base_back = lax.dot_general(
        masked_cot.reshape(tok_count, out_width),
        weight,
        (((1,), (1,)), ((), ())),
        preferred_element_type=f32,
    )
    token_grad = (
        scale * base_back + lora_back.reshape(tok_count, width).astype(f32)
    ).astype(bf16)
    return projection, token_grad, down_grad, up_grad


def solution(mesh):
    placed = (
        P(("groups", "dp"), None),
        P(("groups", "dp"), None),
        P("dp", None),
        P(),
        P("groups", "dp", None),
        P("groups", None, None),
        P(("groups", "dp")),
        P(("groups", "dp")),
    )
    return jax.shard_map(
        local,
        mesh=mesh,
        in_specs=placed,
        out_specs=(
            P(("groups", "dp"), None),
            P(("groups", "dp"), None),
            P("groups", "dp", None),
            P("groups", None, "dp"),
        ),
        check_vma=False,
    )
```

```python
import functools

import jax
import jax.numpy as jnp
from jax import lax
from jax.experimental import pallas as pl
from jax.experimental.pallas import tpu as pltpu
from jax.sharding import PartitionSpec as P

adapter_scale = 2.0
NT = (((1,), (1,)), ((), ()))
TN = (((0,), (0,)), ((), ()))


def exchange(
    n, slot, rank,
    lens_ref, own_idx_ref, scale_ref, tok_ref, cot_ref, w_ref, down_ref, up_ref,
    proj_ref, tig_ref, idx_all, drecv, urecv,
    wbuf, od, csend, dsend, usend, idx_send, idx_sm, mc_ref, g_ref, acc, rk,
    local_sem, idx_s, idx_r, c_s, c_r, d_s, d_r, u_s, u_r, ring_s, ring_r, twin_s, twin_r,
):
    f32, bf16 = jnp.float32, jnp.bfloat16
    me = lax.axis_index("dp")
    rows, width = tok_ref.shape
    seqs = rows // slot
    depth = w_ref.shape[0]
    quarter, half = depth // 4, depth // 2
    chips = n // 2
    side = chips // 2
    core = lax.rem(me, 2)
    twin = me + 1 - 2 * core
    chip = me // 2
    pz, py = chip // 2, lax.rem(chip, 2)
    pos = pz + py * (2 * side - 1 - 2 * pz)

    def chip_at(p):
        p = lax.rem(p + 2 * chips, chips)
        y = p // side
        z = p + y * (2 * side - 1 - 2 * p)
        return 2 * z + y

    ahead = chip_at(pos + 1) * 2 + core
    behind = chip_at(pos - 1) * 2 + core

    def remote(src, dst, s, r, dev):
        return pltpu.make_async_remote_copy(
            src_ref=src, dst_ref=dst, send_sem=s, recv_sem=r,
            device_id={"dp": dev}, device_id_type=pl.DeviceIdType.MESH,
        )

    barrier = pltpu.get_barrier_semaphore()

    @pl.loop(1, n)
    def _(j):
        pl.semaphore_signal(
            barrier, inc=1, device_id={"dp": lax.rem(me + j, n)},
            device_id_type=pl.DeviceIdType.MESH,
        )

    lane = lax.broadcasted_iota(jnp.int32, (8, 128), 1)
    tile = jnp.zeros((8, 128), jnp.int32)
    for s in range(seqs):
        tile = jnp.where(lane == s, own_idx_ref[s], tile)
    idx_send[...] = tile
    pl.semaphore_wait(barrier, n - 1)

    def shard_of(q, t):
        return chip_at(pos - t if q < 2 else pos + t) * 2 + core

    def rows_of(shard, q):
        return pl.ds(pl.multiple_of(shard * depth + q * quarter, quarter), quarter)

    def ring_copy(q, t):
        at = rows_of(shard_of(q, t), q)
        return remote(wbuf.at[at], wbuf.at[at], ring_s.at[q, t], ring_r.at[q, t],
                      ahead if q < 2 else behind)

    def twin_copy(q, t):
        at = rows_of(shard_of(q, t), q)
        return remote(wbuf.at[at], wbuf.at[at], twin_s.at[q, t], twin_r.at[q, t], twin)

    def ring_wait(q, t):
        at = rows_of(shard_of(q, t), q)
        remote(wbuf.at[at], wbuf.at[at], ring_s.at[q, t - 1], ring_r.at[q, t - 1],
               ahead if q < 2 else behind).wait_recv()

    def twin_wait(q, t):
        at = rows_of(shard_of(q, t) + 1 - 2 * core, q)
        at = rows_of(shard_of(q, t) + 1 - 2 * core, q)
        remote(wbuf.at[at], wbuf.at[at], twin_s.at[q, t], twin_r.at[q, t], twin).wait_recv()

    own_rows = pl.ds(pl.multiple_of(me * depth, depth), depth)
    own = pltpu.make_async_copy(w_ref, wbuf.at[own_rows], local_sem.at[0])
    own.start()
    own.wait()
    for q in (0, 2, 1, 3):
        ring_copy(q, 0).start()
    for q in range(4):
        twin_copy(q, 0).start()

    def idx_copy(j, block):
        return remote(idx_send, idx_all.at[block], idx_s.at[j], idx_r.at[j], lax.rem(me + j, n))

    @pl.loop(1, n)
    def _(j):
        idx_copy(j, me).start()

    idx_own = pltpu.make_async_copy(idx_send, idx_all.at[me], local_sem.at[1])
    idx_own.start()

    row = lax.broadcasted_iota(jnp.int32, (rows, 1), 0)
    live = row < lens_ref[0]
    for s in range(1, seqs):
        live = live | ((row >= s * slot) & (row < s * slot + lens_ref[s]))
    mc = jnp.where(live, cot_ref[...].astype(f32), 0.0).astype(bf16)
    mc_ref[...] = mc
    r2 = lax.broadcasted_iota(jnp.int32, (rows, seqs * rank), 0)
    c2 = lax.broadcasted_iota(jnp.int32, (rows, seqs * rank), 1)
    diag = (r2 < slot) & (c2 < rank)
    for s in range(1, seqs):
        diag = diag | ((r2 >= s * slot) & (r2 < (s + 1) * slot)
                       & (c2 >= s * rank) & (c2 < (s + 1) * rank))
    up2 = jnp.concatenate([up_ref[own_idx_ref[s]] for s in range(seqs)], axis=0)
    g = adapter_scale * lax.dot_general(mc, up2, NT, preferred_element_type=f32)
    g_ref[...] = jnp.where(diag, g, 0.0).astype(bf16)

    idx_own.wait()

    @pl.loop(1, n)
    def _(j):
        idx_copy(j, lax.rem(me - j + n, n)).wait_recv()

    to_smem = pltpu.make_async_copy(idx_all, idx_sm, local_sem.at[1])
    to_smem.start()
    to_smem.wait()

    def c_copy(j, block):
        dev = lax.rem(me + j, n)
        return remote(csend.at[dev], od.at[block], c_s.at[j], c_r.at[j], dev)

    for s in range(seqs):
        od[me, pl.ds(s * rank, rank), :] = down_ref[own_idx_ref[s]]

    @pl.loop(1, n)
    def _(j):
        dev = lax.rem(me + j, n)
        for s in range(seqs):
            csend[dev, pl.ds(s * rank, rank), :] = down_ref[idx_sm[dev, 0, s]]
        c_copy(j, me).start()

    def forward(t, last):
        for q in (0, 2, 1, 3):
            ring_wait(q, t)
            if not last:
                ring_copy(q, t).start()
            twin_copy(q, t).start()

    def column(shard, h):
        return pl.ds(pl.multiple_of(shard * depth + h * half, half), half)

    def fwd(shard, h):
        at = column(shard, h)
        acc[...] += jnp.dot(tok_ref[:, at], wbuf[at, :], preferred_element_type=f32)

    def bwd(shard, h):
        at = column(shard, h)
        back = lax.dot_general(mc_ref[...], wbuf[at, :], NT, preferred_element_type=f32)
        lora = jnp.dot(g_ref[...], od[shard, :, pl.ds(h * half, half)], preferred_element_type=f32)
        tig_ref[:, at] = (scale_ref[0] * back + lora.astype(bf16).astype(f32)).astype(bf16)

    def own_part(t, fn):
        for h in range(2):
            fn(shard_of(2 * h, t), h)

    def twin_part(t, fn):
        for h in range(2):
            fn(shard_of(2 * h, t) + 1 - 2 * core, h)

    def twin_arrive(t):
        for q in range(4):
            twin_wait(q, t)

    def d_copy(j, block):
        dev = lax.rem(me + j, n)
        return remote(dsend.at[dev], drecv.at[block], d_s.at[j], d_r.at[j], dev)

    def d_term(dev):
        at = pl.ds(pl.multiple_of(dev * depth, depth), depth)
        dsend[dev] = lax.dot_general(g_ref[...], tok_ref[:, at], TN, preferred_element_type=f32)

    def d_range(first, last):
        @pl.loop(first, last)
        def _(j):
            d_term(lax.rem(me + j, n))
            d_copy(j, me).start()

    acc[...] = jnp.zeros_like(acc)
    forward(1, False)
    d_range(1, n // 2)
    d_term(me)
    d_own = pltpu.make_async_copy(dsend.at[me], drecv.at[me], local_sem.at[2])
    d_own.start()
    forward(2, False)
    d_range(n // 2, n)
    own_part(0, fwd)
    own_part(1, fwd)
    twin_arrive(0)
    twin_part(0, fwd)
    own_part(2, fwd)
    twin_arrive(1)
    twin_part(1, fwd)
    forward(3, False)
    own_part(3, fwd)
    twin_arrive(2)
    twin_part(2, fwd)

    @pl.loop(1, n)
    def _(j):
        c_copy(j, lax.rem(me - j + n, n)).wait_recv()

    rk[...] = jnp.zeros_like(rk)

    @pl.loop(0, n)
    def _(b):
        at = pl.ds(pl.multiple_of(b * depth, depth), depth)
        rk[...] += lax.dot_general(tok_ref[:, at], od[b], NT, preferred_element_type=f32)

    rv = jnp.where(diag, rk[...], 0.0).astype(bf16)
    up_t = lax.dot_general(mc_ref[...], rv, TN, preferred_element_type=f32)
    cols = usend.shape[1]
    for b in range(n):
        usend[b] = up_t[b * cols:(b + 1) * cols, :]

    def u_copy(j, block):
        dev = lax.rem(me + j, n)
        return remote(usend.at[dev], urecv.at[block], u_s.at[j], u_r.at[j], dev)

    @pl.loop(1, n)
    def _(j):
        u_copy(j, me).start()

    u_own = pltpu.make_async_copy(usend.at[me], urecv.at[me], local_sem.at[3])
    u_own.start()
    adapter_out = jnp.dot(rv, up2, preferred_element_type=f32)

    def both(shard, h):
        fwd(shard, h)
        bwd(shard, h)

    forward(4, False)

    @pl.loop(0, 4)
    def _(t):
        own_part(t, bwd)

    @pl.loop(0, 3)
    def _(t):
        twin_part(t, bwd)

    @pl.loop(4, chips - 1)
    def _(t):
        twin_arrive(t - 1)
        own_part(t, both)
        twin_part(t - 1, both)

        @pl.when(t < chips - 2)
        def _():
            forward(t + 1, False)

    forward(chips - 1, True)
    own_part(chips - 1, both)
    twin_arrive(chips - 2)
    twin_part(chips - 2, both)
    twin_arrive(chips - 1)
    twin_part(chips - 1, both)
    out = scale_ref[0] * acc[...] + adapter_scale * adapter_out
    proj_ref[...] = jnp.where(live, out, 0.0).astype(bf16)

    d_own.wait()
    u_own.wait()

    @pl.loop(1, n)
    def _(j):
        back = lax.rem(me - j + n, n)
        d_copy(j, back).wait_recv()
        u_copy(j, back).wait_recv()
        idx_copy(j, me).wait_send()
        c_copy(j, me).wait_send()
        d_copy(j, me).wait_send()
        u_copy(j, me).wait_send()

    @pl.loop(0, chips)
    def _(t):
        for q in range(4):
            twin_copy(q, t).wait_send()

    @pl.loop(0, chips - 1)
    def _(t):
        for q in range(4):
            ring_copy(q, t).wait_send()


def gather_adapters(idx_ref, d_ref, out_ref):
    out_ref[...] = jnp.zeros_like(out_ref)

    @pl.loop(0, d_ref.shape[0])
    def _(k):
        i = idx_ref[k]
        out_ref[i] = out_ref[i] + d_ref[k]


def local_ring(
    n,
    tokens,
    cotangent,
    frozen_weight,
    frozen_scale,
    adapter_down_weight,
    adapter_up_weight,
    sequence_adapter,
    sequence_token_length,
):
    f32, bf16 = jnp.float32, jnp.bfloat16
    rows, width = tokens.shape
    seqs = sequence_adapter.shape[0]
    slot = rows // seqs
    adapters, depth, rank = adapter_down_weight.shape
    out_width = frozen_weight.shape[1]
    cols = out_width // n
    chips = n // 2
    sr = seqs * rank
    total = n * seqs
    vmem = pl.BlockSpec(memory_space=pltpu.VMEM)
    smem = pl.BlockSpec(memory_space=pltpu.SMEM)
    hbm = pl.BlockSpec(memory_space=pl.ANY)
    dma = pltpu.SemaphoreType.DMA
    proj, tig, idx_all, drecv, urecv = pl.pallas_call(
        functools.partial(exchange, n, slot, rank),
        out_shape=(
            jax.ShapeDtypeStruct((rows, out_width), bf16),
            jax.ShapeDtypeStruct((rows, width), bf16),
            jax.ShapeDtypeStruct((n, 8, 128), jnp.int32),
            jax.ShapeDtypeStruct((n, sr, depth), f32),
            jax.ShapeDtypeStruct((n, cols, sr), f32),
        ),
        in_specs=[smem, smem, smem, vmem, vmem, vmem, vmem, vmem],
        out_specs=(vmem, vmem, hbm, hbm, hbm),
        scratch_shapes=[
            pltpu.VMEM((width, out_width), bf16),
            pltpu.VMEM((n, sr, depth), bf16),
            pltpu.VMEM((n, sr, depth), bf16),
            pltpu.VMEM((n, sr, depth), f32),
            pltpu.VMEM((n, cols, sr), f32),
            pltpu.VMEM((8, 128), jnp.int32),
            pltpu.SMEM((n, 8, 128), jnp.int32),
            pltpu.VMEM((rows, out_width), bf16),
            pltpu.VMEM((rows, sr), bf16),
            pltpu.VMEM((rows, out_width), f32),
            pltpu.VMEM((rows, sr), f32),
            dma((4,)),
            dma((n,)), dma((n,)), dma((n,)), dma((n,)),
            dma((n,)), dma((n,)), dma((n,)), dma((n,)),
            dma((4, chips)), dma((4, chips)), dma((4, chips)), dma((4, chips)),
        ],
        compiler_params=pltpu.CompilerParams(
            collective_id=0, has_side_effects=True, vmem_limit_bytes=48 * 2**20
        ),
        cost_estimate=pl.CostEstimate(
            flops=4 * rows * width * out_width, bytes_accessed=2 * rows * width * 2,
            transcendentals=0,
        ),
    )(
        sequence_token_length, sequence_adapter, frozen_scale, tokens, cotangent,
        frozen_weight, jnp.swapaxes(adapter_down_weight, 1, 2), adapter_up_weight,
    )
    every_index = idx_all[:, 0, :seqs].reshape(total)
    down_grad = pl.pallas_call(
        gather_adapters,
        out_shape=jax.ShapeDtypeStruct((adapters, rank, depth), f32),
        in_specs=[smem, vmem],
        out_specs=vmem,
        compiler_params=pltpu.CompilerParams(vmem_limit_bytes=16 * 2**20),
    )(every_index, drecv.reshape(total, rank, depth))
    select = (every_index[None, :] == jnp.arange(adapters, dtype=jnp.int32)[:, None]).astype(f32)
    up_seq = jnp.transpose(urecv.reshape(n, cols, seqs, rank), (0, 2, 3, 1)).reshape(total, rank * cols)
    up_grad = (
        adapter_scale * jnp.dot(select, up_seq, precision=lax.Precision.HIGHEST)
    ).reshape(adapters, rank, cols)
    return proj, tig, jnp.swapaxes(down_grad, 1, 2), up_grad

def local(
    tokens,
    cotangent,
    frozen_weight,
    frozen_scale,
    adapter_down_weight,
    adapter_up_weight,
    sequence_adapter,
    sequence_token_length,
):
    f32, bf16 = jnp.float32, jnp.bfloat16
    tok_count, width = tokens.shape
    seqs = sequence_adapter.shape[0]
    slot = tok_count // seqs
    adapters, shard_width, rank = adapter_down_weight.shape
    out_width = frozen_weight.shape[1]
    n = lax.axis_size("dp")
    scale = frozen_scale[0]

    every_index = lax.all_gather(sequence_adapter, "dp", axis=0, tiled=True)
    total = every_index.shape[0]
    weight = lax.all_gather(frozen_weight, "dp", axis=0, tiled=True)

    down_t = jnp.swapaxes(adapter_down_weight, 1, 2)
    chosen = down_t[every_index].reshape(total * rank, shard_width)
    own_down = lax.all_to_all(chosen, "dp", split_axis=0, concat_axis=1, tiled=True)
    own_down = own_down.reshape(seqs, rank, width)

    positions = lax.broadcasted_iota(jnp.int32, (seqs, slot), 1)
    live = (positions < sequence_token_length[:, None])[:, :, None]
    masked_cot = jnp.where(
        live, cotangent.reshape(seqs, slot, out_width), jnp.zeros((), bf16)
    )
    own_up = adapter_up_weight[sequence_adapter]
    grad_rank = (
        adapter_scale
        * jnp.einsum("spo,sro->spr", masked_cot, own_up, preferred_element_type=f32)
    ).astype(bf16)
    tokens_seq = tokens.reshape(seqs, slot, width)

    down_terms = jnp.einsum(
        "spr,spc->src", grad_rank, tokens_seq, preferred_element_type=f32
    )
    down_all = lax.all_to_all(
        down_terms.reshape(seqs * rank, width), "dp", split_axis=1, concat_axis=0, tiled=True
    )

    rank_vals = jnp.einsum(
        "spc,src->spr", tokens_seq, own_down, preferred_element_type=f32
    ).astype(bf16)
    up_terms = jnp.einsum(
        "spr,spo->sro", rank_vals, masked_cot, preferred_element_type=f32
    )
    up_all = lax.all_to_all(
        up_terms.reshape(seqs * rank, out_width), "dp", split_axis=1, concat_axis=0, tiled=True
    )

    select = (every_index[None, :] == jnp.arange(adapters, dtype=jnp.int32)[:, None]).astype(f32)
    down_grad = jnp.dot(
        select, down_all.reshape(total, rank * shard_width), precision=lax.Precision.HIGHEST
    ).reshape(adapters, rank, shard_width)
    down_grad = jnp.swapaxes(down_grad, 1, 2)
    up_grad = (
        adapter_scale
        * jnp.dot(
            select, up_all.reshape(total, rank * (out_width // n)), precision=lax.Precision.HIGHEST
        )
    ).reshape(adapters, rank, out_width // n)

    adapter_out = jnp.einsum("spr,sro->spo", rank_vals, own_up, preferred_element_type=f32)
    base_out = jnp.dot(tokens, weight, preferred_element_type=f32)
    combined = scale * base_out.reshape(seqs, slot, out_width) + adapter_scale * adapter_out
    projection = jnp.where(live, combined, 0.0).astype(bf16).reshape(tok_count, out_width)

    lora_back = jnp.einsum("spr,src->spc", grad_rank, own_down, preferred_element_type=f32).astype(bf16)
    base_back = lax.dot_general(
        masked_cot.reshape(tok_count, out_width),
        weight,
        (((1,), (1,)), ((), ())),
        preferred_element_type=f32,
    )
    token_grad = (
        scale * base_back + lora_back.reshape(tok_count, width).astype(f32)
    ).astype(bf16)
    return projection, token_grad, down_grad, up_grad


def solution(mesh):
    placed = (
        P(("groups", "dp"), None),
        P(("groups", "dp"), None),
        P("dp", None),
        P(),
        P("groups", "dp", None),
        P("groups", None, None),
        P(("groups", "dp")),
        P(("groups", "dp")),
    )
    n = mesh.shape["dp"]
    ring = n % 4 == 0 and n >= 12 and n <= 32
    return jax.shard_map(
        functools.partial(local_ring, n) if ring else local,
        mesh=mesh,
        in_specs=placed,
        out_specs=(
            P(("groups", "dp"), None),
            P(("groups", "dp"), None),
            P("groups", "dp", None),
            P("groups", None, "dp"),
        ),
        check_vma=False,
    )
```

```python
import functools

import jax
import jax.numpy as jnp
from jax import lax
from jax.experimental import pallas as pl
from jax.experimental.pallas import tpu as pltpu
from jax.sharding import PartitionSpec as P

adapter_scale = 2.0
NT = (((1,), (1,)), ((), ()))
TN = (((0,), (0,)), ((), ()))


def exchange(
    n, slot, rank,
    lens_ref, own_idx_ref, scale_ref, tok_hbm, cot_hbm, w_ref, down_hbm, up_hbm,
    proj_ref, tig_hbm, idx_all, drecv, urecv,
    tok_ref, cot_ref, down_ref, up_ref, tig_ref, wbuf, od, csend, dsend, usend, idx_send, idx_sm, mc_ref, g_ref, acc, rk,
    local_sem, idx_s, idx_r, c_s, c_r, d_s, d_r, u_s, u_r, ring_s, ring_r, twin_s, twin_r, x_s, x_r, xt_s, xt_r, load_sem, store_sem,
):
    f32, bf16 = jnp.float32, jnp.bfloat16
    me = lax.axis_index("dp")
    rows, width = tok_ref.shape
    seqs = rows // slot
    depth = w_ref.shape[0]
    half = depth // 2
    shared, single = half * 3 // 8, half * 5 // 16
    plane = lax.axis_index("groups")
    chips = n // 2
    side = chips // 2
    core = lax.rem(me, 2)
    twin = me + 1 - 2 * core
    chip = me // 2
    pz, py = chip // 2, lax.rem(chip, 2)
    pos = pz + py * (2 * side - 1 - 2 * pz)

    def chip_at(p):
        p = lax.rem(p + 2 * chips, chips)
        y = p // side
        z = p + y * (2 * side - 1 - 2 * p)
        return 2 * z + y

    ahead = chip_at(pos + 1) * 2 + core
    behind = chip_at(pos - 1) * 2 + core

    def remote(src, dst, s, r, dev):
        return pltpu.make_async_remote_copy(
            src_ref=src, dst_ref=dst, send_sem=s, recv_sem=r,
            device_id={"dp": dev}, device_id_type=pl.DeviceIdType.MESH,
        )

    own_rows = pl.ds(pl.multiple_of(me * depth, depth), depth)
    loads = [
        pltpu.make_async_copy(a, b, load_sem.at[i])
        for i, (a, b) in enumerate((
            (w_ref, wbuf.at[own_rows]), (cot_hbm, cot_ref), (up_hbm, up_ref),
            (down_hbm, down_ref), (tok_hbm, tok_ref),
        ))
    ]
    for load in loads:
        load.start()

    barrier = pltpu.get_barrier_semaphore()
    pl.semaphore_signal(
        barrier, inc=1, device_id={"groups": 1 - plane}, device_id_type=pl.DeviceIdType.MESH
    )

    @pl.loop(1, n)
    def _(j):
        pl.semaphore_signal(
            barrier, inc=1, device_id={"dp": lax.rem(me + j, n)},
            device_id_type=pl.DeviceIdType.MESH,
        )

    lane = lax.broadcasted_iota(jnp.int32, (8, 128), 1)
    tile = jnp.zeros((8, 128), jnp.int32)
    for s in range(seqs):
        tile = jnp.where(lane == s, own_idx_ref[s], tile)
    idx_send[...] = tile
    pl.semaphore_wait(barrier, n)

    def shard_of(q, t):
        return chip_at(pos - t if q < 2 else pos + t) * 2 + core

    def rows_of(shard, q):
        if q % 2 == 0:
            return pl.ds(pl.multiple_of(shard * depth + q // 2 * half, 16), shared)
        at = shard * depth + q // 2 * half + shared + plane * single
        return pl.ds(pl.multiple_of(at, 16), single)

    def other_rows(shard, d):
        at = shard * depth + d * half + shared + (1 - plane) * single
        return pl.ds(pl.multiple_of(at, 16), single)

    def ring_copy(q, t):
        at = rows_of(shard_of(q, t), q)
        return remote(wbuf.at[at], wbuf.at[at], ring_s.at[q, t], ring_r.at[q, t],
                      ahead if q < 2 else behind)

    def twin_copy(q, t):
        at = rows_of(shard_of(q, t), q)
        return remote(wbuf.at[at], wbuf.at[at], twin_s.at[q, t], twin_r.at[q, t], twin)

    def x_copy(d, t, at):
        return pltpu.make_async_remote_copy(
            src_ref=wbuf.at[at], dst_ref=wbuf.at[at], send_sem=x_s.at[d, t],
            recv_sem=x_r.at[d, t], device_id={"groups": 1 - plane},
            device_id_type=pl.DeviceIdType.MESH,
        )

    def x_send(d, t):
        return x_copy(d, t, rows_of(shard_of(2 * d, t), 2 * d + 1))

    def xt_copy(d, t):
        at = other_rows(shard_of(2 * d, t), d)
        return remote(wbuf.at[at], wbuf.at[at], xt_s.at[d, t], xt_r.at[d, t], twin)

    def ring_wait(q, t):
        at = rows_of(shard_of(q, t), q)
        remote(wbuf.at[at], wbuf.at[at], ring_s.at[q, t - 1], ring_r.at[q, t - 1],
               ahead if q < 2 else behind).wait_recv()

    def twin_wait(q, t):
        at = rows_of(shard_of(q, t) + 1 - 2 * core, q)
        remote(wbuf.at[at], wbuf.at[at], twin_s.at[q, t], twin_r.at[q, t], twin).wait_recv()

    def xt_wait(d, t):
        at = other_rows(shard_of(2 * d, t) + 1 - 2 * core, d)
        remote(wbuf.at[at], wbuf.at[at], xt_s.at[d, t], xt_r.at[d, t], twin).wait_recv()

    def x_step(t):
        for d in range(2):
            x_copy(d, t, other_rows(shard_of(2 * d, t), d)).wait_recv()
            xt_copy(d, t).start()

    loads[0].wait()

    def idx_copy(j, block):
        return remote(idx_send, idx_all.at[block], idx_s.at[j], idx_r.at[j], lax.rem(me + j, n))

    @pl.loop(1, n)
    def _(j):
        idx_copy(j, me).start()

    for q in (0, 2, 1, 3):
        ring_copy(q, 0).start()
    for q in range(4):
        twin_copy(q, 0).start()
    for d in range(2):
        xt_copy(d, 0).start()
    idx_own = pltpu.make_async_copy(idx_send, idx_all.at[me], local_sem.at[1])
    idx_own.start()

    loads[1].wait()
    loads[2].wait()
    row = lax.broadcasted_iota(jnp.int32, (rows, 1), 0)
    live = row < lens_ref[0]
    for s in range(1, seqs):
        live = live | ((row >= s * slot) & (row < s * slot + lens_ref[s]))
    mc = jnp.where(live, cot_ref[...].astype(f32), 0.0).astype(bf16)
    mc_ref[...] = mc
    r2 = lax.broadcasted_iota(jnp.int32, (rows, seqs * rank), 0)
    c2 = lax.broadcasted_iota(jnp.int32, (rows, seqs * rank), 1)
    diag = (r2 < slot) & (c2 < rank)
    for s in range(1, seqs):
        diag = diag | ((r2 >= s * slot) & (r2 < (s + 1) * slot)
                       & (c2 >= s * rank) & (c2 < (s + 1) * rank))
    up2 = jnp.concatenate([up_ref[own_idx_ref[s]] for s in range(seqs)], axis=0)
    g = adapter_scale * lax.dot_general(mc, up2, NT, preferred_element_type=f32)
    g_ref[...] = jnp.where(diag, g, 0.0).astype(bf16)

    idx_own.wait()

    @pl.loop(1, n)
    def _(j):
        idx_copy(j, lax.rem(me - j + n, n)).wait_recv()

    to_smem = pltpu.make_async_copy(idx_all, idx_sm, local_sem.at[1])
    to_smem.start()
    to_smem.wait()

    def c_copy(j, block):
        dev = lax.rem(me + j, n)
        return remote(csend.at[dev], od.at[block], c_s.at[j], c_r.at[j], dev)

    loads[3].wait()
    for s in range(seqs):
        od[me, pl.ds(s * rank, rank), :] = down_ref[own_idx_ref[s]]

    @pl.loop(1, n)
    def _(j):
        dev = lax.rem(me + j, n)
        for s in range(seqs):
            csend[dev, pl.ds(s * rank, rank), :] = down_ref[idx_sm[dev, 0, s]]
        c_copy(j, me).start()

    def forward(t, last):
        for q in (0, 2, 1, 3):
            ring_wait(q, t)
            if not last:
                ring_copy(q, t).start()
            if q % 2:
                x_send(q // 2, t).start()
            twin_copy(q, t).start()

    def column(shard, h):
        return pl.ds(pl.multiple_of(shard * depth + h * half, half), half)

    def fwd(shard, h):
        at = column(shard, h)
        acc[...] += jnp.dot(tok_ref[:, at], wbuf[at, :], preferred_element_type=f32)

    def bwd(shard, h):
        at = column(shard, h)
        back = lax.dot_general(mc_ref[...], wbuf[at, :], NT, preferred_element_type=f32)
        lora = jnp.dot(g_ref[...], od[shard, :, pl.ds(h * half, half)], preferred_element_type=f32)
        tig_ref[:, at] = (scale_ref[0] * back + lora.astype(bf16).astype(f32)).astype(bf16)

    def own_part(t, fn):
        for h in range(2):
            fn(shard_of(2 * h, t), h)

    def twin_part(t, fn):
        for h in range(2):
            fn(shard_of(2 * h, t) + 1 - 2 * core, h)

    def twin_arrive(t):
        for q in range(4):
            twin_wait(q, t)
        for d in range(2):
            xt_wait(d, t)

    def d_copy(j, block):
        dev = lax.rem(me + j, n)
        return remote(dsend.at[dev], drecv.at[block], d_s.at[j], d_r.at[j], dev)

    def d_term(dev):
        at = pl.ds(pl.multiple_of(dev * depth, depth), depth)
        dsend[dev] = lax.dot_general(g_ref[...], tok_ref[:, at], TN, preferred_element_type=f32)

    def d_range(first, last):
        @pl.loop(first, last)
        def _(j):
            d_term(lax.rem(me + j, n))
            d_copy(j, me).start()

    acc[...] = jnp.zeros_like(acc)
    loads[4].wait()
    per = n // 4
    forward(1, False)
    d_range(1, per)
    forward(2, False)
    x_step(1)
    d_range(per, 2 * per)
    own_part(0, fwd)
    own_part(1, fwd)
    twin_arrive(0)
    twin_part(0, fwd)
    forward(3, False)
    x_step(2)
    d_range(2 * per, 3 * per)
    own_part(2, fwd)
    twin_arrive(1)
    twin_part(1, fwd)
    forward(4, False)
    x_step(3)
    d_range(3 * per, n)
    d_term(me)
    d_own = pltpu.make_async_copy(dsend.at[me], drecv.at[me], local_sem.at[2])
    d_own.start()

    @pl.loop(1, n)
    def _(j):
        c_copy(j, lax.rem(me - j + n, n)).wait_recv()

    rk[...] = jnp.zeros_like(rk)

    @pl.loop(0, n)
    def _(b):
        at = pl.ds(pl.multiple_of(b * depth, depth), depth)
        rk[...] += lax.dot_general(tok_ref[:, at], od[b], NT, preferred_element_type=f32)

    rv = jnp.where(diag, rk[...], 0.0).astype(bf16)
    up_t = lax.dot_general(mc_ref[...], rv, TN, preferred_element_type=f32)
    cols = usend.shape[1]
    for b in range(n):
        usend[b] = up_t[b * cols:(b + 1) * cols, :]

    def u_copy(j, block):
        dev = lax.rem(me + j, n)
        return remote(usend.at[dev], urecv.at[block], u_s.at[j], u_r.at[j], dev)

    @pl.loop(1, n)
    def _(j):
        u_copy(j, me).start()

    u_own = pltpu.make_async_copy(usend.at[me], urecv.at[me], local_sem.at[3])
    u_own.start()
    adapter_out = jnp.dot(rv, up2, preferred_element_type=f32)

    def both(shard, h):
        fwd(shard, h)
        bwd(shard, h)

    @pl.loop(0, 3)
    def _(t):
        own_part(t, bwd)

    @pl.loop(0, 2)
    def _(t):
        twin_part(t, bwd)

    @pl.loop(4, chips - 1)
    def _(t):
        own_part(t - 1, both)
        twin_arrive(t - 2)
        twin_part(t - 2, both)

        @pl.when(t < chips - 2)
        def _():
            forward(t + 1, False)

        @pl.when(t == chips - 2)
        def _():
            forward(chips - 1, True)

        x_step(t)

    own_part(chips - 2, both)
    twin_arrive(chips - 3)
    twin_part(chips - 3, both)
    x_step(chips - 1)
    own_part(chips - 1, both)
    twin_arrive(chips - 2)
    twin_part(chips - 2, both)
    twin_arrive(chips - 1)
    twin_part(chips - 1, both)
    store = pltpu.make_async_copy(tig_ref, tig_hbm, store_sem.at[0])
    store.start()
    out = scale_ref[0] * acc[...] + adapter_scale * adapter_out
    proj_ref[...] = jnp.where(live, out, 0.0).astype(bf16)

    store.wait()
    d_own.wait()
    u_own.wait()

    @pl.loop(1, n)
    def _(j):
        back = lax.rem(me - j + n, n)
        d_copy(j, back).wait_recv()
        u_copy(j, back).wait_recv()
        idx_copy(j, me).wait_send()
        c_copy(j, me).wait_send()
        d_copy(j, me).wait_send()
        u_copy(j, me).wait_send()

    @pl.loop(0, chips)
    def _(t):
        for q in range(4):
            twin_copy(q, t).wait_send()
        for d in range(2):
            xt_copy(d, t).wait_send()

    @pl.loop(1, chips)
    def _(t):
        for d in range(2):
            x_send(d, t).wait_send()

    @pl.loop(0, chips - 1)
    def _(t):
        for q in range(4):
            ring_copy(q, t).wait_send()


def gather_adapters(idx_ref, d_ref, tig_ref, out_ref, tig_out, held, sems):
    parts = sems.shape[1]
    size = tig_ref.shape[0] // parts
    loads, stores = [], []
    for i in range(parts):
        at = pl.ds(i * size, size)
        loads.append(pltpu.make_async_copy(tig_ref.at[at], held.at[at], sems.at[0, i]))
        stores.append(pltpu.make_async_copy(held.at[at], tig_out.at[at], sems.at[1, i]))
    for load in loads:
        load.start()
    out_ref[...] = jnp.zeros_like(out_ref)

    for load, store in zip(loads, stores):
        load.wait()
        store.start()

    @pl.loop(0, d_ref.shape[0])
    def _(k):
        i = idx_ref[k]
        out_ref[i] = out_ref[i] + d_ref[k]

    for store in stores:
        store.wait()


def local_ring(
    n,
    tokens,
    cotangent,
    frozen_weight,
    frozen_scale,
    adapter_down_weight,
    adapter_up_weight,
    sequence_adapter,
    sequence_token_length,
):
    f32, bf16 = jnp.float32, jnp.bfloat16
    rows, width = tokens.shape
    seqs = sequence_adapter.shape[0]
    slot = rows // seqs
    adapters, depth, rank = adapter_down_weight.shape
    out_width = frozen_weight.shape[1]
    cols = out_width // n
    chips = n // 2
    sr = seqs * rank
    total = n * seqs
    vmem = pl.BlockSpec(memory_space=pltpu.VMEM)
    smem = pl.BlockSpec(memory_space=pltpu.SMEM)
    hbm = pl.BlockSpec(memory_space=pl.ANY)
    dma = pltpu.SemaphoreType.DMA
    proj, tig, idx_all, drecv, urecv = pl.pallas_call(
        functools.partial(exchange, n, slot, rank),
        out_shape=(
            jax.ShapeDtypeStruct((rows, out_width), bf16),
            jax.ShapeDtypeStruct((rows, width), bf16),
            jax.ShapeDtypeStruct((n, 8, 128), jnp.int32),
            jax.ShapeDtypeStruct((n, sr, depth), f32),
            jax.ShapeDtypeStruct((n, cols, sr), f32),
        ),
        in_specs=[smem, smem, smem, hbm, hbm, hbm, hbm, hbm],
        out_specs=(vmem, hbm, hbm, hbm, hbm),
        scratch_shapes=[
            pltpu.VMEM((rows, width), bf16),
            pltpu.VMEM((rows, out_width), bf16),
            pltpu.VMEM((adapters, rank, depth), bf16),
            pltpu.VMEM((adapters, rank, out_width), bf16),
            pltpu.VMEM((rows, width), bf16),
            pltpu.VMEM((width, out_width), bf16),
            pltpu.VMEM((n, sr, depth), bf16),
            pltpu.VMEM((n, sr, depth), bf16),
            pltpu.VMEM((n, sr, depth), f32),
            pltpu.VMEM((n, cols, sr), f32),
            pltpu.VMEM((8, 128), jnp.int32),
            pltpu.SMEM((n, 8, 128), jnp.int32),
            pltpu.VMEM((rows, out_width), bf16),
            pltpu.VMEM((rows, sr), bf16),
            pltpu.VMEM((rows, out_width), f32),
            pltpu.VMEM((rows, sr), f32),
            dma((4,)),
            dma((n,)), dma((n,)), dma((n,)), dma((n,)),
            dma((n,)), dma((n,)), dma((n,)), dma((n,)),
            dma((4, chips)), dma((4, chips)), dma((4, chips)), dma((4, chips)),
            dma((2, chips)), dma((2, chips)), dma((2, chips)), dma((2, chips)),
            dma((5,)), dma((1,)),
        ],
        compiler_params=pltpu.CompilerParams(
            collective_id=0, has_side_effects=True, vmem_limit_bytes=60 * 2**20
        ),
        cost_estimate=pl.CostEstimate(
            flops=4 * rows * width * out_width, bytes_accessed=2 * rows * width * 2,
            transcendentals=0,
        ),
    )(
        sequence_token_length, sequence_adapter, frozen_scale, tokens, cotangent,
        frozen_weight, jnp.swapaxes(adapter_down_weight, 1, 2), adapter_up_weight,
    )
    every_index = idx_all[:, 0, :seqs].reshape(total)
    down_grad, tig = pl.pallas_call(
        gather_adapters,
        out_shape=(
            jax.ShapeDtypeStruct((adapters, rank, depth), f32),
            jax.ShapeDtypeStruct((rows, width), bf16),
        ),
        in_specs=[smem, vmem, hbm],
        out_specs=(vmem, hbm),
        scratch_shapes=[pltpu.VMEM((rows, width), bf16), dma((2, 8))],
        compiler_params=pltpu.CompilerParams(vmem_limit_bytes=60 * 2**20),
    )(every_index, drecv.reshape(total, rank, depth), tig)
    select = (every_index[None, :] == jnp.arange(adapters, dtype=jnp.int32)[:, None]).astype(f32)
    up_seq = jnp.transpose(urecv.reshape(n, cols, seqs, rank), (0, 2, 3, 1)).reshape(total, rank * cols)
    up_grad = (
        adapter_scale * jnp.dot(select, up_seq, precision=lax.Precision.HIGHEST)
    ).reshape(adapters, rank, cols)
    return proj, tig, jnp.swapaxes(down_grad, 1, 2), up_grad

def local(
    tokens,
    cotangent,
    frozen_weight,
    frozen_scale,
    adapter_down_weight,
    adapter_up_weight,
    sequence_adapter,
    sequence_token_length,
):
    f32, bf16 = jnp.float32, jnp.bfloat16
    tok_count, width = tokens.shape
    seqs = sequence_adapter.shape[0]
    slot = tok_count // seqs
    adapters, shard_width, rank = adapter_down_weight.shape
    out_width = frozen_weight.shape[1]
    n = lax.axis_size("dp")
    scale = frozen_scale[0]

    every_index = lax.all_gather(sequence_adapter, "dp", axis=0, tiled=True)
    total = every_index.shape[0]
    weight = lax.all_gather(frozen_weight, "dp", axis=0, tiled=True)

    down_t = jnp.swapaxes(adapter_down_weight, 1, 2)
    chosen = down_t[every_index].reshape(total * rank, shard_width)
    own_down = lax.all_to_all(chosen, "dp", split_axis=0, concat_axis=1, tiled=True)
    own_down = own_down.reshape(seqs, rank, width)

    positions = lax.broadcasted_iota(jnp.int32, (seqs, slot), 1)
    live = (positions < sequence_token_length[:, None])[:, :, None]
    masked_cot = jnp.where(
        live, cotangent.reshape(seqs, slot, out_width), jnp.zeros((), bf16)
    )
    own_up = adapter_up_weight[sequence_adapter]
    grad_rank = (
        adapter_scale
        * jnp.einsum("spo,sro->spr", masked_cot, own_up, preferred_element_type=f32)
    ).astype(bf16)
    tokens_seq = tokens.reshape(seqs, slot, width)

    down_terms = jnp.einsum(
        "spr,spc->src", grad_rank, tokens_seq, preferred_element_type=f32
    )
    down_all = lax.all_to_all(
        down_terms.reshape(seqs * rank, width), "dp", split_axis=1, concat_axis=0, tiled=True
    )

    rank_vals = jnp.einsum(
        "spc,src->spr", tokens_seq, own_down, preferred_element_type=f32
    ).astype(bf16)
    up_terms = jnp.einsum(
        "spr,spo->sro", rank_vals, masked_cot, preferred_element_type=f32
    )
    up_all = lax.all_to_all(
        up_terms.reshape(seqs * rank, out_width), "dp", split_axis=1, concat_axis=0, tiled=True
    )

    select = (every_index[None, :] == jnp.arange(adapters, dtype=jnp.int32)[:, None]).astype(f32)
    down_grad = jnp.dot(
        select, down_all.reshape(total, rank * shard_width), precision=lax.Precision.HIGHEST
    ).reshape(adapters, rank, shard_width)
    down_grad = jnp.swapaxes(down_grad, 1, 2)
    up_grad = (
        adapter_scale
        * jnp.dot(
            select, up_all.reshape(total, rank * (out_width // n)), precision=lax.Precision.HIGHEST
        )
    ).reshape(adapters, rank, out_width // n)

    adapter_out = jnp.einsum("spr,sro->spo", rank_vals, own_up, preferred_element_type=f32)
    base_out = jnp.dot(tokens, weight, preferred_element_type=f32)
    combined = scale * base_out.reshape(seqs, slot, out_width) + adapter_scale * adapter_out
    projection = jnp.where(live, combined, 0.0).astype(bf16).reshape(tok_count, out_width)

    lora_back = jnp.einsum("spr,src->spc", grad_rank, own_down, preferred_element_type=f32).astype(bf16)
    base_back = lax.dot_general(
        masked_cot.reshape(tok_count, out_width),
        weight,
        (((1,), (1,)), ((), ())),
        preferred_element_type=f32,
    )
    token_grad = (
        scale * base_back + lora_back.reshape(tok_count, width).astype(f32)
    ).astype(bf16)
    return projection, token_grad, down_grad, up_grad


def solution(mesh):
    placed = (
        P(("groups", "dp"), None),
        P(("groups", "dp"), None),
        P("dp", None),
        P(),
        P("groups", "dp", None),
        P("groups", None, None),
        P(("groups", "dp")),
        P(("groups", "dp")),
    )
    n = mesh.shape["dp"]
    ring = n == 16 and mesh.shape["groups"] == 2
    return jax.shard_map(
        functools.partial(local_ring, n) if ring else local,
        mesh=mesh,
        in_specs=placed,
        out_specs=(
            P(("groups", "dp"), None),
            P(("groups", "dp"), None),
            P("groups", "dp", None),
            P("groups", None, "dp"),
        ),
        check_vma=False,
    )
```

```python
import functools

import jax
import jax.numpy as jnp
from jax import lax
from jax.experimental import pallas as pl
from jax.experimental.pallas import tpu as pltpu
from jax.sharding import PartitionSpec as P

adapter_scale = 2.0
NT = (((1,), (1,)), ((), ()))
TN = (((0,), (0,)), ((), ()))


def exchange(
    n, slot, rank,
    lens_ref, own_idx_ref, scale_ref, tok_hbm, cot_hbm, w_ref, down_hbm, up_hbm,
    proj_ref, tig_hbm, idx_all, drecv, urecv,
    tok_ref, cot_ref, down_ref, up_ref, tig_ref, wbuf, od, csend, dsend, usend, idx_send, idx_sm, mc_ref, g_ref, acc, rk,
    local_sem, idx_s, idx_r, c_s, c_r, d_s, d_r, u_s, u_r, ring_s, ring_r, twin_s, twin_r, x_s, x_r, xt_s, xt_r, load_sem, store_sem,
):
    f32, bf16 = jnp.float32, jnp.bfloat16
    me = lax.axis_index("dp")
    rows, width = tok_ref.shape
    seqs = rows // slot
    depth = w_ref.shape[0]
    half = depth // 2
    shared, single = half // 4, half * 3 // 8
    plane = lax.axis_index("groups")
    chips = n // 2
    side = chips // 2
    core = lax.rem(me, 2)
    twin = me + 1 - 2 * core
    chip = me // 2
    pz, py = chip // 2, lax.rem(chip, 2)
    pos = pz + py * (2 * side - 1 - 2 * pz)

    def chip_at(p):
        p = lax.rem(p + 2 * chips, chips)
        y = p // side
        z = p + y * (2 * side - 1 - 2 * p)
        return 2 * z + y

    ahead = chip_at(pos + 1) * 2 + core
    behind = chip_at(pos - 1) * 2 + core

    def remote(src, dst, s, r, dev):
        return pltpu.make_async_remote_copy(
            src_ref=src, dst_ref=dst, send_sem=s, recv_sem=r,
            device_id={"dp": dev}, device_id_type=pl.DeviceIdType.MESH,
        )

    own_rows = pl.ds(pl.multiple_of(me * depth, depth), depth)
    loads = [
        pltpu.make_async_copy(a, b, load_sem.at[i])
        for i, (a, b) in enumerate((
            (w_ref, wbuf.at[own_rows]), (cot_hbm, cot_ref), (up_hbm, up_ref),
            (down_hbm, down_ref), (tok_hbm, tok_ref),
        ))
    ]
    for load in loads:
        load.start()

    barrier = pltpu.get_barrier_semaphore()
    pl.semaphore_signal(
        barrier, inc=1, device_id={"groups": 1 - plane}, device_id_type=pl.DeviceIdType.MESH
    )

    @pl.loop(1, n)
    def _(j):
        pl.semaphore_signal(
            barrier, inc=1, device_id={"dp": lax.rem(me + j, n)},
            device_id_type=pl.DeviceIdType.MESH,
        )

    lane = lax.broadcasted_iota(jnp.int32, (8, 128), 1)
    tile = jnp.zeros((8, 128), jnp.int32)
    for s in range(seqs):
        tile = jnp.where(lane == s, own_idx_ref[s], tile)
    idx_send[...] = tile
    pl.semaphore_wait(barrier, n)

    def shard_of(q, t):
        return chip_at(pos - t if q < 2 else pos + t) * 2 + core

    def rows_of(shard, q):
        if q % 2 == 0:
            return pl.ds(pl.multiple_of(shard * depth + q // 2 * half, 16), shared)
        at = shard * depth + q // 2 * half + shared + plane * single
        return pl.ds(pl.multiple_of(at, 16), single)

    def other_rows(shard, d):
        at = shard * depth + d * half + shared + (1 - plane) * single
        return pl.ds(pl.multiple_of(at, 16), single)

    def ring_copy(q, t):
        at = rows_of(shard_of(q, t), q)
        return remote(wbuf.at[at], wbuf.at[at], ring_s.at[q, t], ring_r.at[q, t],
                      ahead if q < 2 else behind)

    def twin_copy(q, t):
        at = rows_of(shard_of(q, t), q)
        return remote(wbuf.at[at], wbuf.at[at], twin_s.at[q, t], twin_r.at[q, t], twin)

    def x_copy(d, t, at):
        return pltpu.make_async_remote_copy(
            src_ref=wbuf.at[at], dst_ref=wbuf.at[at], send_sem=x_s.at[d, t],
            recv_sem=x_r.at[d, t], device_id={"groups": 1 - plane},
            device_id_type=pl.DeviceIdType.MESH,
        )

    def x_send(d, t):
        return x_copy(d, t, rows_of(shard_of(2 * d, t), 2 * d + 1))

    def xt_copy(d, t):
        at = other_rows(shard_of(2 * d, t), d)
        return remote(wbuf.at[at], wbuf.at[at], xt_s.at[d, t], xt_r.at[d, t], twin)

    def ring_wait(q, t):
        at = rows_of(shard_of(q, t), q)
        remote(wbuf.at[at], wbuf.at[at], ring_s.at[q, t - 1], ring_r.at[q, t - 1],
               ahead if q < 2 else behind).wait_recv()

    def twin_wait(q, t):
        at = rows_of(shard_of(q, t) + 1 - 2 * core, q)
        remote(wbuf.at[at], wbuf.at[at], twin_s.at[q, t], twin_r.at[q, t], twin).wait_recv()

    def xt_wait(d, t):
        at = other_rows(shard_of(2 * d, t) + 1 - 2 * core, d)
        remote(wbuf.at[at], wbuf.at[at], xt_s.at[d, t], xt_r.at[d, t], twin).wait_recv()

    def x_step(t):
        for d in range(2):
            x_copy(d, t, other_rows(shard_of(2 * d, t), d)).wait_recv()
            xt_copy(d, t).start()

    loads[0].wait()

    def idx_copy(j, block):
        return remote(idx_send, idx_all.at[block], idx_s.at[j], idx_r.at[j], lax.rem(me + j, n))

    @pl.loop(1, n)
    def _(j):
        idx_copy(j, me).start()

    for q in (0, 2, 1, 3):
        ring_copy(q, 0).start()
    for q in range(4):
        twin_copy(q, 0).start()
    for d in range(2):
        xt_copy(d, 0).start()
    idx_own = pltpu.make_async_copy(idx_send, idx_all.at[me], local_sem.at[1])
    idx_own.start()

    loads[1].wait()
    loads[2].wait()
    row = lax.broadcasted_iota(jnp.int32, (rows, 1), 0)
    live = row < lens_ref[0]
    for s in range(1, seqs):
        live = live | ((row >= s * slot) & (row < s * slot + lens_ref[s]))
    mc = jnp.where(live, cot_ref[...].astype(f32), 0.0).astype(bf16)
    mc_ref[...] = mc
    r2 = lax.broadcasted_iota(jnp.int32, (rows, seqs * rank), 0)
    c2 = lax.broadcasted_iota(jnp.int32, (rows, seqs * rank), 1)
    diag = (r2 < slot) & (c2 < rank)
    for s in range(1, seqs):
        diag = diag | ((r2 >= s * slot) & (r2 < (s + 1) * slot)
                       & (c2 >= s * rank) & (c2 < (s + 1) * rank))
    up2 = jnp.concatenate([up_ref[own_idx_ref[s]] for s in range(seqs)], axis=0)
    g = adapter_scale * lax.dot_general(mc, up2, NT, preferred_element_type=f32)
    g_ref[...] = jnp.where(diag, g, 0.0).astype(bf16)

    def d_copy(j, block):
        dev = lax.rem(me + j, n)
        return remote(dsend.at[dev], drecv.at[block], d_s.at[j], d_r.at[j], dev)

    def d_term(dev):
        at = pl.ds(pl.multiple_of(dev * depth, depth), depth)
        dsend[dev] = lax.dot_general(g_ref[...], tok_ref[:, at], TN, preferred_element_type=f32)

    def d_range(first, last):
        @pl.loop(first, last)
        def _(j):
            d_term(lax.rem(me + j, n))
            d_copy(j, me).start()

    per = n // 4
    loads[4].wait()
    d_range(1, per)

    idx_own.wait()

    @pl.loop(1, n)
    def _(j):
        idx_copy(j, lax.rem(me - j + n, n)).wait_recv()

    to_smem = pltpu.make_async_copy(idx_all, idx_sm, local_sem.at[1])
    to_smem.start()
    to_smem.wait()

    def c_copy(j, block):
        dev = lax.rem(me + j, n)
        return remote(csend.at[dev], od.at[block], c_s.at[j], c_r.at[j], dev)

    loads[3].wait()
    for s in range(seqs):
        od[me, pl.ds(s * rank, rank), :] = down_ref[own_idx_ref[s]]

    @pl.loop(1, n)
    def _(j):
        dev = lax.rem(me + j, n)
        for s in range(seqs):
            csend[dev, pl.ds(s * rank, rank), :] = down_ref[idx_sm[dev, 0, s]]
        c_copy(j, me).start()

    def forward(t, last):
        for q in (0, 2, 1, 3):
            ring_wait(q, t)
            if not last:
                ring_copy(q, t).start()
            if q % 2:
                x_send(q // 2, t).start()
            twin_copy(q, t).start()

    def column(shard, h):
        return pl.ds(pl.multiple_of(shard * depth + h * half, half), half)

    def fwd(shard, h):
        at = column(shard, h)
        acc[...] += jnp.dot(tok_ref[:, at], wbuf[at, :], preferred_element_type=f32)

    def bwd(shard, h):
        at = column(shard, h)
        back = lax.dot_general(mc_ref[...], wbuf[at, :], NT, preferred_element_type=f32)
        lora = jnp.dot(g_ref[...], od[shard, :, pl.ds(h * half, half)], preferred_element_type=f32)
        tig_ref[:, at] = (scale_ref[0] * back + lora.astype(bf16).astype(f32)).astype(bf16)

    def own_part(t, fn):
        for h in range(2):
            fn(shard_of(2 * h, t), h)

    def twin_part(t, fn):
        for h in range(2):
            fn(shard_of(2 * h, t) + 1 - 2 * core, h)

    def twin_arrive(t):
        for q in range(4):
            twin_wait(q, t)
        for d in range(2):
            xt_wait(d, t)

    acc[...] = jnp.zeros_like(acc)
    forward(1, False)
    d_range(per, 2 * per)
    forward(2, False)
    x_step(1)
    d_range(2 * per, 3 * per)
    own_part(0, fwd)
    own_part(1, fwd)
    twin_arrive(0)
    twin_part(0, fwd)
    forward(3, False)
    x_step(2)
    d_range(3 * per, n)
    own_part(2, fwd)
    twin_arrive(1)
    twin_part(1, fwd)
    forward(4, False)
    x_step(3)
    d_term(me)
    d_own = pltpu.make_async_copy(dsend.at[me], drecv.at[me], local_sem.at[2])
    d_own.start()

    @pl.loop(1, n)
    def _(j):
        c_copy(j, lax.rem(me - j + n, n)).wait_recv()

    rk[...] = jnp.zeros_like(rk)

    @pl.loop(0, n)
    def _(b):
        at = pl.ds(pl.multiple_of(b * depth, depth), depth)
        rk[...] += lax.dot_general(tok_ref[:, at], od[b], NT, preferred_element_type=f32)

    rv = jnp.where(diag, rk[...], 0.0).astype(bf16)
    up_t = lax.dot_general(mc_ref[...], rv, TN, preferred_element_type=f32)
    cols = usend.shape[1]
    for b in range(n):
        usend[b] = up_t[b * cols:(b + 1) * cols, :]

    def u_copy(j, block):
        dev = lax.rem(me + j, n)
        return remote(usend.at[dev], urecv.at[block], u_s.at[j], u_r.at[j], dev)

    @pl.loop(1, n)
    def _(j):
        u_copy(j, me).start()

    u_own = pltpu.make_async_copy(usend.at[me], urecv.at[me], local_sem.at[3])
    u_own.start()
    adapter_out = jnp.dot(rv, up2, preferred_element_type=f32)

    def both(shard, h):
        fwd(shard, h)
        bwd(shard, h)

    @pl.loop(0, 3)
    def _(t):
        own_part(t, bwd)

    @pl.loop(0, 2)
    def _(t):
        twin_part(t, bwd)

    @pl.loop(4, chips - 1)
    def _(t):
        own_part(t - 1, both)
        twin_arrive(t - 2)
        twin_part(t - 2, both)

        @pl.when(t < chips - 2)
        def _():
            forward(t + 1, False)

        @pl.when(t == chips - 2)
        def _():
            forward(chips - 1, True)

        x_step(t)

    own_part(chips - 2, both)
    twin_arrive(chips - 3)
    twin_part(chips - 3, both)
    x_step(chips - 1)
    own_part(chips - 1, both)
    twin_arrive(chips - 2)
    twin_part(chips - 2, both)
    twin_arrive(chips - 1)
    twin_part(chips - 1, both)
    store = pltpu.make_async_copy(tig_ref, tig_hbm, store_sem.at[0])
    store.start()
    out = scale_ref[0] * acc[...] + adapter_scale * adapter_out
    proj_ref[...] = jnp.where(live, out, 0.0).astype(bf16)

    store.wait()
    d_own.wait()
    u_own.wait()

    @pl.loop(1, n)
    def _(j):
        back = lax.rem(me - j + n, n)
        d_copy(j, back).wait_recv()
        u_copy(j, back).wait_recv()
        idx_copy(j, me).wait_send()
        c_copy(j, me).wait_send()
        d_copy(j, me).wait_send()
        u_copy(j, me).wait_send()

    @pl.loop(0, chips)
    def _(t):
        for q in range(4):
            twin_copy(q, t).wait_send()
        for d in range(2):
            xt_copy(d, t).wait_send()

    @pl.loop(1, chips)
    def _(t):
        for d in range(2):
            x_send(d, t).wait_send()

    @pl.loop(0, chips - 1)
    def _(t):
        for q in range(4):
            ring_copy(q, t).wait_send()


def gather_adapters(idx_ref, d_ref, tig_ref, out_ref, tig_out, held, sems):
    parts = sems.shape[1]
    size = tig_ref.shape[0] // parts
    loads, stores = [], []
    for i in range(parts):
        at = pl.ds(i * size, size)
        loads.append(pltpu.make_async_copy(tig_ref.at[at], held.at[at], sems.at[0, i]))
        stores.append(pltpu.make_async_copy(held.at[at], tig_out.at[at], sems.at[1, i]))
    for load in loads:
        load.start()
    out_ref[...] = jnp.zeros_like(out_ref)

    for load, store in zip(loads, stores):
        load.wait()
        store.start()

    @pl.loop(0, d_ref.shape[0])
    def _(k):
        i = idx_ref[k]
        out_ref[i] = out_ref[i] + d_ref[k]

    for store in stores:
        store.wait()


def local_ring(
    n,
    tokens,
    cotangent,
    frozen_weight,
    frozen_scale,
    adapter_down_weight,
    adapter_up_weight,
    sequence_adapter,
    sequence_token_length,
):
    f32, bf16 = jnp.float32, jnp.bfloat16
    rows, width = tokens.shape
    seqs = sequence_adapter.shape[0]
    slot = rows // seqs
    adapters, depth, rank = adapter_down_weight.shape
    out_width = frozen_weight.shape[1]
    cols = out_width // n
    chips = n // 2
    sr = seqs * rank
    total = n * seqs
    vmem = pl.BlockSpec(memory_space=pltpu.VMEM)
    smem = pl.BlockSpec(memory_space=pltpu.SMEM)
    hbm = pl.BlockSpec(memory_space=pl.ANY)
    dma = pltpu.SemaphoreType.DMA
    proj, tig, idx_all, drecv, urecv = pl.pallas_call(
        functools.partial(exchange, n, slot, rank),
        out_shape=(
            jax.ShapeDtypeStruct((rows, out_width), bf16),
            jax.ShapeDtypeStruct((rows, width), bf16),
            jax.ShapeDtypeStruct((n, 8, 128), jnp.int32),
            jax.ShapeDtypeStruct((n, sr, depth), f32),
            jax.ShapeDtypeStruct((n, cols, sr), f32),
        ),
        in_specs=[smem, smem, smem, hbm, hbm, hbm, hbm, hbm],
        out_specs=(vmem, hbm, hbm, hbm, hbm),
        scratch_shapes=[
            pltpu.VMEM((rows, width), bf16),
            pltpu.VMEM((rows, out_width), bf16),
            pltpu.VMEM((adapters, rank, depth), bf16),
            pltpu.VMEM((adapters, rank, out_width), bf16),
            pltpu.VMEM((rows, width), bf16),
            pltpu.VMEM((width, out_width), bf16),
            pltpu.VMEM((n, sr, depth), bf16),
            pltpu.VMEM((n, sr, depth), bf16),
            pltpu.VMEM((n, sr, depth), f32),
            pltpu.VMEM((n, cols, sr), f32),
            pltpu.VMEM((8, 128), jnp.int32),
            pltpu.SMEM((n, 8, 128), jnp.int32),
            pltpu.VMEM((rows, out_width), bf16),
            pltpu.VMEM((rows, sr), bf16),
            pltpu.VMEM((rows, out_width), f32),
            pltpu.VMEM((rows, sr), f32),
            dma((4,)),
            dma((n,)), dma((n,)), dma((n,)), dma((n,)),
            dma((n,)), dma((n,)), dma((n,)), dma((n,)),
            dma((4, chips)), dma((4, chips)), dma((4, chips)), dma((4, chips)),
            dma((2, chips)), dma((2, chips)), dma((2, chips)), dma((2, chips)),
            dma((5,)), dma((1,)),
        ],
        compiler_params=pltpu.CompilerParams(
            collective_id=0, has_side_effects=True, vmem_limit_bytes=60 * 2**20
        ),
        cost_estimate=pl.CostEstimate(
            flops=4 * rows * width * out_width, bytes_accessed=2 * rows * width * 2,
            transcendentals=0,
        ),
    )(
        sequence_token_length, sequence_adapter, frozen_scale, tokens, cotangent,
        frozen_weight, jnp.swapaxes(adapter_down_weight, 1, 2), adapter_up_weight,
    )
    every_index = idx_all[:, 0, :seqs].reshape(total)
    down_grad, tig = pl.pallas_call(
        gather_adapters,
        out_shape=(
            jax.ShapeDtypeStruct((adapters, rank, depth), f32),
            jax.ShapeDtypeStruct((rows, width), bf16),
        ),
        in_specs=[smem, vmem, hbm],
        out_specs=(vmem, hbm),
        scratch_shapes=[pltpu.VMEM((rows, width), bf16), dma((2, 8))],
        compiler_params=pltpu.CompilerParams(vmem_limit_bytes=60 * 2**20),
    )(every_index, drecv.reshape(total, rank, depth), tig)
    select = (every_index[None, :] == jnp.arange(adapters, dtype=jnp.int32)[:, None]).astype(f32)
    up_seq = jnp.transpose(urecv.reshape(n, cols, seqs, rank), (0, 2, 3, 1)).reshape(total, rank * cols)
    up_grad = (
        adapter_scale * jnp.dot(select, up_seq, precision=lax.Precision.HIGHEST)
    ).reshape(adapters, rank, cols)
    return proj, tig, jnp.swapaxes(down_grad, 1, 2), up_grad

def local(
    tokens,
    cotangent,
    frozen_weight,
    frozen_scale,
    adapter_down_weight,
    adapter_up_weight,
    sequence_adapter,
    sequence_token_length,
):
    f32, bf16 = jnp.float32, jnp.bfloat16
    tok_count, width = tokens.shape
    seqs = sequence_adapter.shape[0]
    slot = tok_count // seqs
    adapters, shard_width, rank = adapter_down_weight.shape
    out_width = frozen_weight.shape[1]
    n = lax.axis_size("dp")
    scale = frozen_scale[0]

    every_index = lax.all_gather(sequence_adapter, "dp", axis=0, tiled=True)
    total = every_index.shape[0]
    weight = lax.all_gather(frozen_weight, "dp", axis=0, tiled=True)

    down_t = jnp.swapaxes(adapter_down_weight, 1, 2)
    chosen = down_t[every_index].reshape(total * rank, shard_width)
    own_down = lax.all_to_all(chosen, "dp", split_axis=0, concat_axis=1, tiled=True)
    own_down = own_down.reshape(seqs, rank, width)

    positions = lax.broadcasted_iota(jnp.int32, (seqs, slot), 1)
    live = (positions < sequence_token_length[:, None])[:, :, None]
    masked_cot = jnp.where(
        live, cotangent.reshape(seqs, slot, out_width), jnp.zeros((), bf16)
    )
    own_up = adapter_up_weight[sequence_adapter]
    grad_rank = (
        adapter_scale
        * jnp.einsum("spo,sro->spr", masked_cot, own_up, preferred_element_type=f32)
    ).astype(bf16)
    tokens_seq = tokens.reshape(seqs, slot, width)

    down_terms = jnp.einsum(
        "spr,spc->src", grad_rank, tokens_seq, preferred_element_type=f32
    )
    down_all = lax.all_to_all(
        down_terms.reshape(seqs * rank, width), "dp", split_axis=1, concat_axis=0, tiled=True
    )

    rank_vals = jnp.einsum(
        "spc,src->spr", tokens_seq, own_down, preferred_element_type=f32
    ).astype(bf16)
    up_terms = jnp.einsum(
        "spr,spo->sro", rank_vals, masked_cot, preferred_element_type=f32
    )
    up_all = lax.all_to_all(
        up_terms.reshape(seqs * rank, out_width), "dp", split_axis=1, concat_axis=0, tiled=True
    )

    select = (every_index[None, :] == jnp.arange(adapters, dtype=jnp.int32)[:, None]).astype(f32)
    down_grad = jnp.dot(
        select, down_all.reshape(total, rank * shard_width), precision=lax.Precision.HIGHEST
    ).reshape(adapters, rank, shard_width)
    down_grad = jnp.swapaxes(down_grad, 1, 2)
    up_grad = (
        adapter_scale
        * jnp.dot(
            select, up_all.reshape(total, rank * (out_width // n)), precision=lax.Precision.HIGHEST
        )
    ).reshape(adapters, rank, out_width // n)

    adapter_out = jnp.einsum("spr,sro->spo", rank_vals, own_up, preferred_element_type=f32)
    base_out = jnp.dot(tokens, weight, preferred_element_type=f32)
    combined = scale * base_out.reshape(seqs, slot, out_width) + adapter_scale * adapter_out
    projection = jnp.where(live, combined, 0.0).astype(bf16).reshape(tok_count, out_width)

    lora_back = jnp.einsum("spr,src->spc", grad_rank, own_down, preferred_element_type=f32).astype(bf16)
    base_back = lax.dot_general(
        masked_cot.reshape(tok_count, out_width),
        weight,
        (((1,), (1,)), ((), ())),
        preferred_element_type=f32,
    )
    token_grad = (
        scale * base_back + lora_back.reshape(tok_count, width).astype(f32)
    ).astype(bf16)
    return projection, token_grad, down_grad, up_grad


def solution(mesh):
    placed = (
        P(("groups", "dp"), None),
        P(("groups", "dp"), None),
        P("dp", None),
        P(),
        P("groups", "dp", None),
        P("groups", None, None),
        P(("groups", "dp")),
        P(("groups", "dp")),
    )
    n = mesh.shape["dp"]
    ring = n == 16 and mesh.shape["groups"] == 2
    return jax.shard_map(
        functools.partial(local_ring, n) if ring else local,
        mesh=mesh,
        in_specs=placed,
        out_specs=(
            P(("groups", "dp"), None),
            P(("groups", "dp"), None),
            P("groups", "dp", None),
            P("groups", None, "dp"),
        ),
        check_vma=False,
    )
```
